768 devices in a mesh: wide: 192 (over x, y_hi, z), narrow: 4 (over y_lo, core).
Axes of the slice: x: 4, y: 8 (y_hi: 4, y_lo: 2; y = y_hi * 2 + y_lo), z: 12, core: 2. Of those that a mesh axis runs over, the one named last changes fastest.
Arguments:
- image_embeds: bfloat16 [3072, 1152], P(('wide', 'narrow')), may hold values from -16 to 16
- text_embeds: bfloat16 [3072, 1152], P(('wide', 'narrow')), may hold values from -16 to 16
- log_scale: float32 [1], replicated, may hold values from 1.5 to 2.5
- bias: float32 [1], replicated, may hold values from -2 to 0
Outputs:
- row_loss: float32 [3072], P(('wide', 'narrow'))
- image_grad: float32 [3072, 1152], P(('wide', 'narrow'))
- text_grad: float32 [3072, 1152], P(('wide', 'narrow'))
The draws below stay inside these ranges and needn't reach their ends.
All inputs are finite; a program needn't handle non-finite values.
Results may differ from the reference program's by a relative error of at most 0.0014.
Values may be sent and summed in bfloat16 or wider, within the bound.
No kernel may reach another device: no remote copies, remote signals or barrier semaphores. Data moves between devices by JAX's collectives and lax.ppermute only.
A program may use at most 32 MiB of HBM per device.

```python
import math
import jax
import jax.numpy as jnp
from jax import lax

D = 1152
ROWS_DEV = 4
BATCH = 3072
N_NARROW = 4


def shared_rows(key):
    keys = jax.random.split(key, 4)
    groups = max(BATCH // 32, 2)
    centers = jnp.clip(jax.random.normal(keys[0], (groups, D), jnp.float32), -4.0, 4.0)
    member = jax.random.randint(keys[1], (BATCH,), 0, groups)
    weight = jax.random.uniform(keys[2], (BATCH, 1), jnp.float32, 0.5, 1.5)
    noise = jnp.clip(jax.random.normal(keys[3], (BATCH, D), jnp.float32), -4.0, 4.0)
    return weight * centers[member] + noise


def own_rows(key):
    keys = jax.random.split(key, 2)
    own = jnp.clip(jax.random.normal(keys[0], (BATCH, D), jnp.float32), -4.0, 4.0)
    scales = jnp.exp(jax.random.uniform(keys[1], (BATCH, 1), jnp.float32, math.log(0.5), math.log(5.0)))
    return (own, scales)


def draw_image_embeds(key, part):
    base = shared_rows(key)
    key = jax.random.fold_in(key, 11)
    own, scales = own_rows(key)
    return jnp.clip(scales * (0.8 * base + 0.6 * own), -16.0, 16.0).astype(jnp.bfloat16)


def draw_text_embeds(key, part):
    base = shared_rows(key)
    key = jax.random.fold_in(key, 23)
    own, scales = own_rows(key)
    return jnp.clip(scales * (0.8 * base + 0.6 * own), -16.0, 16.0).astype(jnp.bfloat16)


def setup_inputs(seed: int = 0) -> dict:
    key_of = jax.random.split(jax.random.key(seed), 5)
    return {
        "image_embeds": draw_image_embeds(jax.random.fold_in(key_of[4], 71), 0),
        "text_embeds": draw_text_embeds(jax.random.fold_in(key_of[4], 71), 0),
        "log_scale": jnp.clip(jax.random.uniform(key_of[2], (1,), jnp.float32, 1.5, 2.5), 1.5, 2.5),
        "bias": jnp.clip(jax.random.uniform(key_of[3], (1,), jnp.float32, -2.0, 0.0), -2.0, 0.0),
    }


epsilon = 1e-06

def unit_rows(embeds):
    values = embeds.astype(jnp.float32)
    inverse = lax.rsqrt(lax.optimization_barrier(jnp.sum(values * values, axis=1, keepdims=True)) + epsilon)
    unit = values * inverse
    return (inverse, unit, unit.astype(jnp.bfloat16))

def backward_unit(inverse, unit, upstream):
    return inverse * (upstream - unit * lax.optimization_barrier(jnp.sum(unit * upstream, axis=1, keepdims=True)))

def reference(image_embeds, text_embeds, log_scale, bias):
    image_inverse, image_unit, image_low = unit_rows(image_embeds)
    text_inverse, text_unit, text_low = unit_rows(text_embeds)
    scale_value = jnp.exp(log_scale[0])
    bias_value = bias[0]
    batch = image_embeds.shape[0]
    group_rows = N_NARROW * ROWS_DEV
    blocks = batch // group_rows
    columns = jnp.arange(batch, dtype=jnp.int32)

    def block_terms(text_acc, block_index):
        first_row = (block_index * group_rows).astype(jnp.int32)
        image_block = lax.dynamic_slice_in_dim(image_low, first_row, group_rows, 0)
        logits = scale_value * jnp.dot(image_block, text_low.T, preferred_element_type=jnp.float32) + bias_value
        row_ids = first_row + jnp.arange(group_rows, dtype=jnp.int32)
        labels = jnp.where(row_ids[:, None] == columns[None, :], 1.0, -1.0).astype(jnp.float32)
        loss_rows = lax.optimization_barrier(jnp.sum(jax.nn.softplus(-labels * logits), axis=1)) / batch
        coefs = (-scale_value * labels * jax.nn.sigmoid(-labels * logits)).astype(jnp.bfloat16)
        image_part = jnp.dot(coefs, text_low, preferred_element_type=jnp.float32)
        text_acc = text_acc + jnp.dot(coefs.T, image_block, preferred_element_type=jnp.float32)
        return (text_acc, (loss_rows, image_part))
    text_part, (loss_rows, image_parts) = lax.scan(block_terms, jnp.zeros((batch, D), jnp.float32), jnp.arange(blocks, dtype=jnp.int32))
    image_part = image_parts.reshape(batch, D)
    row_loss = loss_rows.reshape(batch)
    image_grad = backward_unit(image_inverse, image_unit, image_part)
    text_grad = backward_unit(text_inverse, text_unit, text_part)
    return (row_loss, image_grad, text_grad)
```

```python
import jax
import jax.numpy as jnp
from jax import lax
from jax.sharding import Mesh
from jax.sharding import PartitionSpec as P

epsilon = 1e-06
AXES = ("x", "yh", "z", "yl", "c")
SIZES = (4, 4, 12, 2, 2)
IMAGE = ("z", "c")
TEXT = ("x", "yh", "yl")


def unit_rows(embeds):
    values = embeds.astype(jnp.float32)
    inverse = lax.rsqrt(jnp.sum(values * values, axis=1, keepdims=True) + epsilon)
    unit = values * inverse
    return (inverse, unit, unit.astype(jnp.bfloat16))


def backward_unit(inverse, unit, upstream):
    return inverse * (upstream - unit * jnp.sum(unit * upstream, axis=1, keepdims=True))


def share_rows(rows, axes):
    count = lax.axis_size(axes)
    copies = jnp.broadcast_to(rows[None], (count,) + rows.shape)
    return lax.all_to_all(copies, axes, 0, 0, tiled=True).reshape(count * rows.shape[0], -1)


def sum_rows(parts, axes):
    count = lax.axis_size(axes)
    pieces = parts.reshape(count, parts.shape[0] // count, parts.shape[1])
    return jnp.sum(lax.all_to_all(pieces, axes, 0, 0, tiled=True), axis=0)


def on_device(image_embeds, text_embeds, log_scale, bias):
    rows, width = image_embeds.shape
    batch = rows * lax.axis_size(AXES)
    image_inverse, image_unit, image_low = unit_rows(image_embeds)
    text_inverse, text_unit, text_low = unit_rows(text_embeds)
    scale_value = jnp.exp(log_scale[0])
    bias_value = bias[0]
    images = share_rows(image_low, IMAGE)
    texts = share_rows(text_low, TEXT)
    row_ids = jnp.arange(images.shape[0], dtype=jnp.int32)[:, None] - rows * lax.axis_index(IMAGE)
    column_ids = jnp.arange(texts.shape[0], dtype=jnp.int32)[None, :] - rows * lax.axis_index(TEXT)
    positive = (row_ids == column_ids) & (row_ids >= 0) & (row_ids < rows)
    raw_logits = lax.dot_general(
        images, texts, (((1,), (1,)), ((), ())), preferred_element_type=jnp.float32
    )
    logits = scale_value * raw_logits + bias_value
    labels = jnp.where(positive, 1.0, -1.0).astype(jnp.float32)
    losses = jnp.sum(jax.nn.softplus(-labels * logits), axis=1, keepdims=True)
    coefs = (-scale_value * labels * jax.nn.sigmoid(-labels * logits)).astype(jnp.bfloat16)
    image_part = jnp.dot(coefs, texts, preferred_element_type=jnp.float32)
    text_part = lax.dot_general(
        coefs, images, (((0,), (0,)), ((), ())), preferred_element_type=jnp.float32
    )
    packed = jnp.concatenate([image_part, jnp.broadcast_to(losses, (losses.shape[0], 128))], axis=1)
    image_sum = sum_rows(packed, IMAGE)
    text_sum = sum_rows(text_part, TEXT)
    row_loss = image_sum[:, width] / batch
    image_grad = backward_unit(image_inverse, image_unit, image_sum[:, :width])
    text_grad = backward_unit(text_inverse, text_unit, text_sum)
    return (row_loss, image_grad, text_grad)


def solution(mesh):
    fine = Mesh(mesh.devices.reshape(SIZES), AXES)
    in_specs = (P(AXES, None), P(AXES, None), P(), P())
    out_specs = (P(AXES), P(AXES, None), P(AXES, None))
    return jax.shard_map(
        on_device, mesh=fine, in_specs=in_specs, out_specs=out_specs, check_vma=False
    )
```

```python
import jax
import jax.numpy as jnp
from jax import lax
from jax.sharding import Mesh
from jax.sharding import PartitionSpec as P

epsilon = 1e-06
AXES = ("x", "yh", "z", "yl", "c")
SIZES = (4, 4, 12, 2, 2)
IMAGE = ("c", "z")
TEXT = ("x", "yh", "yl")
IMAGE_GAIN = 16.0
TEXT_GAIN = 32.0


def unit_rows(embeds):
    values = embeds.astype(jnp.float32)
    inverse = lax.rsqrt(jnp.sum(values * values, axis=1, keepdims=True) + epsilon)
    unit = values * inverse
    return (inverse, unit, unit.astype(jnp.bfloat16))


def backward_unit(inverse, unit, upstream):
    return inverse * (upstream - unit * jnp.sum(unit * upstream, axis=1, keepdims=True))


def share_text(rows):
    count = lax.axis_size(TEXT)
    copies = jnp.broadcast_to(rows[None], (count,) + rows.shape)
    return lax.all_to_all(copies, TEXT, 0, 0, tiled=True).reshape(count * rows.shape[0], -1)


def share_images(rows):
    along_z = lax.all_gather(rows, "z", axis=0, tiled=True)
    return lax.all_gather(along_z, "c", axis=0, tiled=True)


def send_rows(pieces, axes):
    count = lax.axis_size(axes)
    pieces = pieces.reshape(count, pieces.shape[0] // count, pieces.shape[1])
    return lax.all_to_all(pieces, axes, 0, 0, tiled=True)


def sum_rows(arrived, gain):
    return jnp.sum(arrived.astype(jnp.float32), axis=0) * (1.0 / gain)


def on_device(image_embeds, text_embeds, log_scale, bias):
    rows, width = image_embeds.shape
    batch = rows * lax.axis_size(AXES)
    text_inverse, text_unit, text_low = unit_rows(text_embeds)
    image_inverse, image_unit, image_low = unit_rows(image_embeds)
    scale_value = jnp.exp(log_scale[0])
    bias_value = bias[0]
    texts = share_text(text_low)
    images = share_images(image_low)
    row_ids = jnp.arange(images.shape[0], dtype=jnp.int32)[:, None] - rows * lax.axis_index(IMAGE)
    column_ids = jnp.arange(texts.shape[0], dtype=jnp.int32)[None, :] - rows * lax.axis_index(TEXT)
    positive = (row_ids == column_ids) & (row_ids >= 0) & (row_ids < rows)
    raw_logits = lax.dot_general(
        images, texts, (((1,), (1,)), ((), ())), preferred_element_type=jnp.float32
    )
    logits = scale_value * raw_logits + bias_value
    labels = jnp.where(positive, 1.0, -1.0).astype(jnp.float32)
    losses = jnp.sum(jax.nn.softplus(-labels * logits), axis=1, keepdims=True)
    coefs = (-scale_value * labels * jax.nn.sigmoid(-labels * logits)).astype(jnp.bfloat16)
    text_part = lax.dot_general(
        coefs, images, (((0,), (0,)), ((), ())), preferred_element_type=jnp.float32
    )
    text_arrived = send_rows((text_part * TEXT_GAIN).astype(jnp.float16), TEXT)
    image_part = jnp.dot(coefs, texts, preferred_element_type=jnp.float32)
    packed = jnp.concatenate([image_part, jnp.broadcast_to(losses, (losses.shape[0], 128))], axis=1)
    both = lax.all_gather(packed, "c", axis=0).reshape(2, 2, packed.shape[0] // 2, -1)
    chip_part = jnp.sum(lax.dynamic_index_in_dim(both, lax.axis_index("c"), 1, keepdims=False), axis=0)
    chip_loss = chip_part[:, width:]
    rest = chip_loss - (chip_loss * IMAGE_GAIN).astype(jnp.float16).astype(jnp.float32) * (1.0 / IMAGE_GAIN)
    upper = jnp.arange(128, dtype=jnp.int32)[None, :] >= 64
    chip_part = jnp.concatenate([chip_part[:, :width], jnp.where(upper, rest, chip_loss)], axis=1)
    image_pieces = (chip_part * IMAGE_GAIN).astype(jnp.float16)
    image_pieces, text_arrived = lax.optimization_barrier((image_pieces, text_arrived))
    image_sum = sum_rows(send_rows(image_pieces, "z"), IMAGE_GAIN)
    text_sum = sum_rows(text_arrived, TEXT_GAIN)
    row_loss = (image_sum[:, width] + image_sum[:, width + 64]) / batch
    image_grad = backward_unit(image_inverse, image_unit, image_sum[:, :width])
    text_grad = backward_unit(text_inverse, text_unit, text_sum)
    return (row_loss, image_grad, text_grad)


def solution(mesh):
    fine = Mesh(mesh.devices.reshape(SIZES), AXES)
    in_specs = (P(AXES, None), P(AXES, None), P(), P())
    out_specs = (P(AXES), P(AXES, None), P(AXES, None))
    return jax.shard_map(
        on_device, mesh=fine, in_specs=in_specs, out_specs=out_specs, check_vma=False
    )
```

```python
import jax
import jax.numpy as jnp
from jax import lax
from jax.sharding import Mesh
from jax.sharding import PartitionSpec as P

epsilon = 1e-06
AXES = ("x", "yh", "z", "yl", "c")
SIZES = (4, 4, 12, 2, 2)
RUN = 3
STRIDE = 2
GAIN = 16.0
LOSS_COLUMNS = 128


def exchange_groups():
    members = {}
    xs, yhs, zs, yls, cs = SIZES
    device = 0
    for x in range(xs):
        for yh in range(yhs):
            for z in range(zs):
                for yl in range(yls):
                    text_key = (0, yh, z // RUN, 0)
                    image_key = (1, x, yl, z % STRIDE)
                    for core, key in enumerate((text_key, image_key)):
                        members.setdefault(key, []).append(device + core)
                    device += cs
    return [members[key] for key in sorted(members)]


def exchange(pieces):
    return lax.all_to_all(pieces, AXES, 0, 0, axis_index_groups=exchange_groups(), tiled=True)


def on_device(image_embeds, text_embeds, log_scale, bias):
    rows, width = image_embeds.shape
    batch = rows * lax.axis_size(AXES)
    x, yh, z, yl, c = [lax.axis_index(name) for name in AXES]
    is_text = c == 0
    chip_rows = 2 * rows
    chip_embeds = lax.all_gather(jnp.concatenate([text_embeds, image_embeds], axis=0), "c", axis=0)
    embeds = jnp.where(is_text, chip_embeds[:, :rows], chip_embeds[:, rows:]).reshape(chip_rows, width)
    values = embeds.astype(jnp.float32)
    inverse = lax.rsqrt(jnp.sum(values * values, axis=1, keepdims=True) + epsilon)
    unit = values * inverse
    low = unit.astype(jnp.bfloat16)
    scale_value = jnp.exp(log_scale[0])
    bias_value = bias[0]
    count = len(exchange_groups()[0])
    own = exchange(jnp.broadcast_to(low[None], (count, chip_rows, width))).reshape(-1, width)
    both = lax.all_gather(own, "c", axis=0)
    other = jnp.where(is_text, both[1], both[0])
    text_place = (x * RUN + z % RUN) * 2 + yl
    image_place = yh * (SIZES[2] // STRIDE) + z // STRIDE
    own_place = jnp.where(is_text, text_place, image_place)
    other_place = jnp.where(is_text, image_place, text_place)
    own_step = jnp.where(is_text, 2 * STRIDE, 1)
    other_step = jnp.where(is_text, 1, 2 * STRIDE)
    own_ids = jnp.arange(own.shape[0], dtype=jnp.int32)[:, None] - chip_rows * own_place
    other_ids = jnp.arange(own.shape[0], dtype=jnp.int32)[None, :] - chip_rows * other_place
    own_twin = own_ids - chip_rows * own_step
    other_twin = other_ids - chip_rows * other_step
    positive = ((own_ids == other_ids) & (own_ids >= 0) & (own_ids < chip_rows)) | (
        (z % RUN == 0) & (own_twin == other_twin) & (own_twin >= 0) & (own_twin < chip_rows)
    )
    counted = jnp.where(z % RUN == RUN - 1, 0.0, 1.0)
    raw_logits = lax.dot_general(
        own, other, (((1,), (1,)), ((), ())), preferred_element_type=jnp.float32
    )
    logits = scale_value * raw_logits + bias_value
    labels = jnp.where(positive, 1.0, -1.0).astype(jnp.float32)
    losses = counted * jnp.sum(jax.nn.softplus(-labels * logits), axis=1, keepdims=True)
    coefs = (-scale_value * counted * labels * jax.nn.sigmoid(-labels * logits)).astype(jnp.bfloat16)
    part = jnp.dot(coefs, other, preferred_element_type=jnp.float32) * GAIN
    losses = losses * GAIN
    rest = losses - losses.astype(jnp.float16).astype(jnp.float32)
    upper = jnp.arange(LOSS_COLUMNS, dtype=jnp.int32)[None, :] >= LOSS_COLUMNS // 2
    packed = jnp.concatenate([part, jnp.where(upper, rest, losses)], axis=1).astype(jnp.float16)
    arrived = exchange(packed.reshape(count, chip_rows, -1))
    total = jnp.sum(arrived.astype(jnp.float32), axis=0) * (1.0 / GAIN)
    upstream = total[:, :width]
    row_loss = (total[:, width:] + jnp.roll(total[:, width:], LOSS_COLUMNS // 2, axis=1)) / batch
    grad = inverse * (upstream - unit * jnp.sum(unit * upstream, axis=1, keepdims=True))
    chip_grads = lax.all_gather(jnp.concatenate([grad, row_loss], axis=1), "c", axis=0)
    text_out = lax.dynamic_slice_in_dim(chip_grads[0], c * rows, rows, 0)
    image_out = lax.dynamic_slice_in_dim(chip_grads[1], c * rows, rows, 0)
    return (image_out[:, width], image_out[:, :width], text_out[:, :width])


def solution(mesh):
    fine = Mesh(mesh.devices.reshape(SIZES), AXES)
    in_specs = (P(AXES, None), P(AXES, None), P(), P())
    out_specs = (P(AXES), P(AXES, None), P(AXES, None))
    return jax.shard_map(
        on_device, mesh=fine, in_specs=in_specs, out_specs=out_specs, check_vma=False
    )
```

```python
import jax
import jax.numpy as jnp
from jax import lax
from jax.sharding import Mesh
from jax.experimental import pallas as pl
from jax.experimental.pallas import tpu as pltpu
from jax.sharding import PartitionSpec as P

epsilon = 1e-06
AXES = ("x", "yh", "z", "yl", "c")
SIZES = (4, 4, 12, 2, 2)
SLAB = 3
GAIN = 16.0
LOSS_COLUMNS = 128


def device_place(device):
    coordinates = []
    for size in reversed(SIZES):
        coordinates.append(device % size)
        device = device // size
    return coordinates[::-1]


def places(x, y, z):
    plane = z % SLAB
    text_place = 2 * z + x % 2
    outer_place = 8 * (x // 2) + y
    middle_place = 16 + 4 * (x // 2) + y // 2
    return (plane, text_place, outer_place, middle_place)


def exchange_groups():
    members = {}
    xs, yhs, zs, yls, cs = SIZES
    device = 0
    for x in range(xs):
        for yh in range(yhs):
            for z in range(zs):
                for yl in range(yls):
                    y = yh * yls + yl
                    plane, text_place, outer_place, middle_place = places(x, y, z)
                    last = (x // 2 + y) % 2 if plane == 1 else plane // 2
                    image_place = middle_place if plane == 1 else outer_place
                    text_key = (0, x // 2, y, 0)
                    image_key = (1, z // SLAB, last, x % 2)
                    for core, key, place in ((0, text_key, text_place), (1, image_key, image_place)):
                        members.setdefault(key, []).append((place, device + core))
                    device += cs
    return [[device for _, device in sorted(members[key])] for key in sorted(members)]


def exchange(pieces):
    return lax.all_to_all(pieces, AXES, 0, 0, axis_index_groups=exchange_groups(), tiled=True)


def on_device(image_embeds, text_embeds, log_scale, bias):
    rows, width = image_embeds.shape
    batch = rows * lax.axis_size(AXES)
    device = lax.axis_index(AXES)
    is_text = device % SIZES[-1] == 0
    chip_rows = 2 * rows
    chip_embeds = lax.all_gather(jnp.concatenate([text_embeds, image_embeds], axis=0), "c", axis=0)
    embeds = jnp.where(is_text, chip_embeds[:, :rows], chip_embeds[:, rows:]).reshape(chip_rows, width)
    values = embeds.astype(jnp.float32)
    inverse = lax.rsqrt(jnp.sum(values * values, axis=1, keepdims=True) + epsilon)
    unit = values * inverse
    low = unit.astype(jnp.bfloat16)
    count = len(exchange_groups()[0])
    pieces = jnp.broadcast_to(low[None], (count, chip_rows, width))
    half_columns = jnp.int32(LOSS_COLUMNS // 2)
    tied = lax.optimization_barrier((pieces, device, log_scale, bias, half_columns))
    own, device, log_scale, bias, half_columns = lax.optimization_barrier(
        (exchange(tied[0]),) + tied[1:]
    )
    scale_value = jnp.exp(log_scale[0])
    bias_value = bias[0]
    x, yh, z, yl, c = device_place(device)
    own_is_text = c == 0
    own = own.reshape(-1, width)
    both = lax.all_gather(own, "c", axis=0)
    other = jnp.where(own_is_text, both[1], both[0])
    y = yh * SIZES[3] + yl
    plane, text_place, image_place, twin_image_place = places(x, y, z)
    twin_text_place = text_place + jnp.where(plane == 0, 2, -2)
    has_twin = plane // 2 == (x // 2 + y) % 2

    def row_ids(place, axis):
        return lax.broadcasted_iota(jnp.int32, (own.shape[0], own.shape[0]), axis) - chip_rows * place

    def same_rows(text, image):
        own_ids = row_ids(jnp.where(own_is_text, text, image), 0)
        other_ids = row_ids(jnp.where(own_is_text, image, text), 1)
        return (own_ids == other_ids) & (own_ids >= 0) & (own_ids < chip_rows)

    positive = same_rows(text_place, image_place) | (
        has_twin & same_rows(twin_text_place, twin_image_place)
    )
    counted = jnp.where(plane == 1, 0.0, 1.0)
    raw_logits = lax.dot_general(
        own, other, (((1,), (1,)), ((), ())), preferred_element_type=jnp.float32
    )
    logits = scale_value * raw_logits + bias_value
    labels = jnp.where(positive, 1.0, -1.0).astype(jnp.float32)
    losses = counted * jnp.sum(jax.nn.softplus(-labels * logits), axis=1, keepdims=True)
    coefs = (-scale_value * counted * labels * jax.nn.sigmoid(-labels * logits)).astype(jnp.bfloat16)
    part = jnp.dot(coefs, other, preferred_element_type=jnp.float32) * GAIN
    losses = losses * GAIN
    rest = losses - losses.astype(jnp.float16).astype(jnp.float32)
    upper = jnp.arange(LOSS_COLUMNS, dtype=jnp.int32)[None, :] >= half_columns
    packed = jnp.concatenate([part, jnp.where(upper, rest, losses)], axis=1).astype(jnp.float16)
    arrived = exchange(packed.reshape(count, chip_rows, -1))
    total = jnp.sum(arrived.astype(jnp.float32), axis=0) * (1.0 / GAIN)
    upstream = total[:, :width]
    row_loss = (total[:, width:] + jnp.roll(total[:, width:], LOSS_COLUMNS // 2, axis=1)) / batch
    grad = inverse * (upstream - unit * jnp.sum(unit * upstream, axis=1, keepdims=True))
    chip_grads = lax.all_gather(jnp.concatenate([grad, row_loss], axis=1), "c", axis=0)
    row_loss, image_grad, text_grad = deal_rows(chip_grads, rows, width)
    return (row_loss.reshape(rows), image_grad, text_grad)


def deal_kernel(chip_ref, loss_ref, image_ref, text_ref):
    rows, width = image_ref.shape
    core = lax.axis_index("c")
    for kind, out_ref in ((0, text_ref), (1, image_ref)):
        out_ref[...] = jnp.where(
            core == 0, chip_ref[kind, :rows, :width], chip_ref[kind, rows:, :width]
        )
    losses = chip_ref[1, :, width:]
    row = lax.broadcasted_iota(jnp.int32, losses.shape, 0)
    column = lax.broadcasted_iota(jnp.int32, losses.shape, 1)
    turned = jnp.sum(jnp.where(row == column + rows * core, losses, 0.0), axis=0, keepdims=True)
    loss_ref[...] = turned[:, :rows]


def deal_rows(chip_grads, rows, width):
    return pl.pallas_call(
        deal_kernel,
        in_specs=[pl.BlockSpec(memory_space=pltpu.VMEM)],
        out_specs=[pl.BlockSpec(memory_space=pltpu.VMEM)] * 3,
        out_shape=[
            jax.ShapeDtypeStruct((1, rows), jnp.float32),
            jax.ShapeDtypeStruct((rows, width), jnp.float32),
            jax.ShapeDtypeStruct((rows, width), jnp.float32),
        ],
        compiler_params=pltpu.CompilerParams(vmem_limit_bytes=2 << 20),
        name="deal_rows",
    )(chip_grads)


def solution(mesh):
    fine = Mesh(mesh.devices.reshape(SIZES), AXES)
    in_specs = (P(AXES, None), P(AXES, None), P(), P())
    out_specs = (P(AXES), P(AXES, None), P(AXES, None))
    return jax.shard_map(
        on_device, mesh=fine, in_specs=in_specs, out_specs=out_specs, check_vma=False
    )
```

```python
import jax
import jax.numpy as jnp
from jax import lax
from jax.sharding import Mesh
from jax.experimental import pallas as pl
from jax.experimental.pallas import tpu as pltpu
from jax.sharding import PartitionSpec as P

epsilon = 1e-06
AXES = ("x", "yh", "z", "yl", "c")
SIZES = (4, 4, 12, 2, 2)
RUN = 3
GAIN = 16.0
LOSS_COLUMNS = 128


def device_place(device):
    coordinates = []
    for size in reversed(SIZES):
        coordinates.append(device % size)
        device = device // size
    return coordinates[::-1]


def places(x, y, z):
    run, step = z // RUN, z % RUN
    last, late = step // 2, run // 2
    half = (last + late) % 2
    text_place = RUN * y + step
    rank = last * (run + 2 * late) + (1 - last) * (2 * run - 2 * late + step)
    return (step, half, text_place, 6 * x + rank)


def exchange_groups():
    members = {}
    xs, yhs, zs, yls, cs = SIZES
    device = 0
    for x in range(xs):
        for yh in range(yhs):
            for z in range(zs):
                for yl in range(yls):
                    y = yh * yls + yl
                    _, half, text_place, image_place = places(x, y, z)
                    text_key = (0, x, z // RUN)
                    image_key = (1, y, half)
                    for core, key, place in ((0, text_key, text_place), (1, image_key, image_place)):
                        members.setdefault(key, []).append((place, device + core))
                    device += cs
    return [[device for _, device in sorted(members[key])] for key in sorted(members)]


def exchange(pieces):
    return lax.all_to_all(pieces, AXES, 0, 0, axis_index_groups=exchange_groups(), tiled=True)


def on_device(image_embeds, text_embeds, log_scale, bias):
    rows, width = image_embeds.shape
    batch = rows * lax.axis_size(AXES)
    device = lax.axis_index(AXES)
    is_text = device % SIZES[-1] == 0
    chip_rows = 2 * rows
    chip_embeds = lax.all_gather(jnp.concatenate([text_embeds, image_embeds], axis=0), "c", axis=0)
    embeds = jnp.where(is_text, chip_embeds[:, :rows], chip_embeds[:, rows:]).reshape(chip_rows, width)
    values = embeds.astype(jnp.float32)
    inverse = lax.rsqrt(jnp.sum(values * values, axis=1, keepdims=True) + epsilon)
    unit = values * inverse
    low = unit.astype(jnp.bfloat16)
    count = len(exchange_groups()[0])
    pieces = jnp.broadcast_to(low[None], (count, chip_rows, width))
    half_columns = jnp.int32(LOSS_COLUMNS // 2)
    tied = lax.optimization_barrier((pieces, device, log_scale, bias, half_columns))
    own, device, log_scale, bias, half_columns = lax.optimization_barrier(
        (exchange(tied[0]),) + tied[1:]
    )
    scale_value = jnp.exp(log_scale[0])
    bias_value = bias[0]
    x, yh, z, yl, c = device_place(device)
    own_is_text = c == 0
    own = own.reshape(-1, width)
    both = lax.all_gather(own, "c", axis=0)
    other = jnp.where(own_is_text, both[1], both[0])
    step, _, text_place, image_place = places(x, yh * SIZES[3] + yl, z)
    has_twin = step == 0

    def row_ids(place, axis):
        return lax.broadcasted_iota(jnp.int32, (own.shape[0], own.shape[0]), axis) - chip_rows * place

    def same_rows(text, image):
        own_ids = row_ids(jnp.where(own_is_text, text, image), 0)
        other_ids = row_ids(jnp.where(own_is_text, image, text), 1)
        return (own_ids == other_ids) & (own_ids >= 0) & (own_ids < chip_rows)

    positive = same_rows(text_place, image_place) | (
        has_twin & same_rows(text_place + 1, image_place + 1)
    )
    counted = jnp.where(step == 1, 0.0, 1.0)
    raw_logits = lax.dot_general(
        own, other, (((1,), (1,)), ((), ())), preferred_element_type=jnp.float32
    )
    logits = scale_value * raw_logits + bias_value
    labels = jnp.where(positive, 1.0, -1.0).astype(jnp.float32)
    losses = counted * jnp.sum(jax.nn.softplus(-labels * logits), axis=1, keepdims=True)
    coefs = (-scale_value * counted * labels * jax.nn.sigmoid(-labels * logits)).astype(jnp.bfloat16)
    part = jnp.dot(coefs, other, preferred_element_type=jnp.float32) * GAIN
    losses = losses * GAIN
    rest = losses - losses.astype(jnp.float16).astype(jnp.float32)
    upper = jnp.arange(LOSS_COLUMNS, dtype=jnp.int32)[None, :] >= half_columns
    packed = jnp.concatenate([part, jnp.where(upper, rest, losses)], axis=1).astype(jnp.float16)
    arrived = exchange(packed.reshape(count, chip_rows, -1))
    total = jnp.sum(arrived.astype(jnp.float32), axis=0) * (1.0 / GAIN)
    upstream = total[:, :width]
    row_loss = (total[:, width:] + jnp.roll(total[:, width:], LOSS_COLUMNS // 2, axis=1)) / batch
    grad = inverse * (upstream - unit * jnp.sum(unit * upstream, axis=1, keepdims=True))
    chip_grads = lax.all_gather(jnp.concatenate([grad, row_loss], axis=1), "c", axis=0)
    row_loss, image_grad, text_grad = deal_rows(chip_grads, rows, width)
    return (row_loss.reshape(rows), image_grad, text_grad)


def deal_kernel(chip_ref, loss_ref, image_ref, text_ref):
    rows, width = image_ref.shape
    core = lax.axis_index("c")
    for kind, out_ref in ((0, text_ref), (1, image_ref)):
        out_ref[...] = jnp.where(
            core == 0, chip_ref[kind, :rows, :width], chip_ref[kind, rows:, :width]
        )
    losses = chip_ref[1, :, width:]
    row = lax.broadcasted_iota(jnp.int32, losses.shape, 0)
    column = lax.broadcasted_iota(jnp.int32, losses.shape, 1)
    turned = jnp.sum(jnp.where(row == column + rows * core, losses, 0.0), axis=0, keepdims=True)
    loss_ref[...] = turned[:, :rows]


def deal_rows(chip_grads, rows, width):
    return pl.pallas_call(
        deal_kernel,
        in_specs=[pl.BlockSpec(memory_space=pltpu.VMEM)],
        out_specs=[pl.BlockSpec(memory_space=pltpu.VMEM)] * 3,
        out_shape=[
            jax.ShapeDtypeStruct((1, rows), jnp.float32),
            jax.ShapeDtypeStruct((rows, width), jnp.float32),
            jax.ShapeDtypeStruct((rows, width), jnp.float32),
        ],
        compiler_params=pltpu.CompilerParams(vmem_limit_bytes=2 << 20),
        name="deal_rows",
    )(chip_grads)


def solution(mesh):
    fine = Mesh(mesh.devices.reshape(SIZES), AXES)
    in_specs = (P(AXES, None), P(AXES, None), P(), P())
    out_specs = (P(AXES), P(AXES, None), P(AXES, None))
    return jax.shard_map(
        on_device, mesh=fine, in_specs=in_specs, out_specs=out_specs, check_vma=False
    )
```

```python
import jax
import jax.numpy as jnp
from jax import lax
from jax.sharding import Mesh
from jax.experimental import pallas as pl
from jax.experimental.pallas import tpu as pltpu
from jax.sharding import PartitionSpec as P

epsilon = 1e-06
AXES = ("x", "yh", "z", "yl", "c")
SIZES = (4, 4, 12, 2, 2)
RUN = 3
GAIN = 16.0
LOSS_COLUMNS = 128


def places(x, y, z):
    run, step = z // RUN, z % RUN
    last, late = step // 2, run // 2
    half = (last + late) % 2
    text_place = RUN * y + step
    rank = last * (run + 2 * late) + (1 - last) * (2 * run - 2 * late + step)
    return (step, half, text_place, 6 * x + rank)


def exchange_groups():
    members = {}
    xs, yhs, zs, yls, cs = SIZES
    device = 0
    for x in range(xs):
        for yh in range(yhs):
            for z in range(zs):
                for yl in range(yls):
                    y = yh * yls + yl
                    _, half, text_place, image_place = places(x, y, z)
                    text_key = (0, x, z // RUN)
                    image_key = (1, y, half)
                    for core, key, place in ((0, text_key, text_place), (1, image_key, image_place)):
                        members.setdefault(key, []).append((place, device + core))
                    device += cs
    return [[device for _, device in sorted(members[key])] for key in sorted(members)]


def exchange(pieces):
    return lax.all_to_all(pieces, AXES, 0, 0, axis_index_groups=exchange_groups(), tiled=True)


def on_device(image_embeds, text_embeds, log_scale, bias):
    rows, width = image_embeds.shape
    batch = rows * lax.axis_size(AXES)
    device = lax.axis_index(AXES)
    is_text = device % SIZES[-1] == 0
    chip_rows = 2 * rows
    chip_embeds = lax.all_gather(jnp.concatenate([text_embeds, image_embeds], axis=0), "c", axis=0)
    embeds = jnp.where(is_text, chip_embeds[:, :rows], chip_embeds[:, rows:]).reshape(chip_rows, width)
    values = embeds.astype(jnp.float32)
    inverse = lax.rsqrt(jnp.sum(values * values, axis=1, keepdims=True) + epsilon)
    unit = values * inverse
    low = unit.astype(jnp.bfloat16)
    count = len(exchange_groups()[0])
    own = exchange(jnp.broadcast_to(low[None], (count, chip_rows, width)))
    both = lax.all_gather(own.reshape(-1, width), "c", axis=0)
    packed = pair_block(both, log_scale, bias, count).astype(jnp.float16)
    arrived = exchange(packed)
    total = jnp.sum(arrived.astype(jnp.float32), axis=0) * (1.0 / GAIN)
    upstream = total[:, :width]
    row_loss = (total[:, width:] + jnp.roll(total[:, width:], LOSS_COLUMNS // 2, axis=1)) / batch
    grad = inverse * (upstream - unit * jnp.sum(unit * upstream, axis=1, keepdims=True))
    chip_grads = lax.all_gather(jnp.concatenate([grad, row_loss], axis=1), "c", axis=0)
    row_loss, image_grad, text_grad = deal_rows(chip_grads, rows, width)
    return (row_loss.reshape(rows), image_grad, text_grad)


def block_kernel(both_ref, log_scale_ref, bias_ref, packed_ref):
    count, chip_rows, _ = packed_ref.shape
    width = both_ref.shape[2]
    x, yh, z, yl, c = [lax.axis_index(name) for name in AXES]
    own, other = both_ref[c], both_ref[1 - c]
    step, _, text_place, image_place = places(x, yh * SIZES[3] + yl, z)
    own_place = jnp.where(c == 0, text_place, image_place)
    other_place = jnp.where(c == 0, image_place, text_place)
    pairs = (own.shape[0], other.shape[0])
    own_ids = lax.broadcasted_iota(jnp.int32, pairs, 0) - chip_rows * own_place
    other_ids = lax.broadcasted_iota(jnp.int32, pairs, 1) - chip_rows * other_place
    chips = jnp.where(step == 0, 2, 1)
    positive = (own_ids == other_ids) & (own_ids >= 0) & (own_ids < chips * chip_rows)
    counted = jnp.where(step == 1, 0.0, 1.0)
    raw_logits = lax.dot_general(
        own, other, (((1,), (1,)), ((), ())), preferred_element_type=jnp.float32
    )
    scale_value = jnp.exp(log_scale_ref[...])
    logits = scale_value * raw_logits + bias_ref[...]
    labels = jnp.where(positive, 1.0, -1.0)
    margins = -labels * logits
    softplus = jnp.maximum(margins, 0.0) + jnp.log1p(jnp.exp(-jnp.abs(margins)))
    losses = (GAIN * counted) * jnp.sum(softplus, axis=1, keepdims=True)
    coefs = ((-counted * scale_value) * labels * jax.nn.sigmoid(margins)).astype(jnp.bfloat16)
    part = jnp.dot(coefs, other, preferred_element_type=jnp.float32) * GAIN
    packed_ref[:, :, :width] = part.reshape(count, chip_rows, width)
    rounded = losses.astype(jnp.bfloat16).astype(jnp.float32)
    column = lax.broadcasted_iota(jnp.int32, (pairs[0], LOSS_COLUMNS), 1)
    columns = jnp.where(column < LOSS_COLUMNS // 2, rounded, losses - rounded)
    packed_ref[:, :, width:] = columns.reshape(count, chip_rows, LOSS_COLUMNS)


def pair_block(both, log_scale, bias, count):
    _, own_rows, width = both.shape
    return pl.pallas_call(
        block_kernel,
        in_specs=[pl.BlockSpec(memory_space=pltpu.VMEM)] * 3,
        out_specs=pl.BlockSpec(memory_space=pltpu.VMEM),
        out_shape=jax.ShapeDtypeStruct((count, own_rows // count, width + LOSS_COLUMNS), jnp.float32),
        compiler_params=pltpu.CompilerParams(vmem_limit_bytes=12 << 20),
        name="pair_block",
    )(both, log_scale.reshape(1, 1), bias.reshape(1, 1))


def deal_kernel(chip_ref, loss_ref, image_ref, text_ref):
    rows, width = image_ref.shape
    core = lax.axis_index("c")
    for kind, out_ref in ((0, text_ref), (1, image_ref)):
        out_ref[...] = jnp.where(
            core == 0, chip_ref[kind, :rows, :width], chip_ref[kind, rows:, :width]
        )
    losses = chip_ref[1, :, width:]
    row = lax.broadcasted_iota(jnp.int32, losses.shape, 0)
    column = lax.broadcasted_iota(jnp.int32, losses.shape, 1)
    turned = jnp.sum(jnp.where(row == column + rows * core, losses, 0.0), axis=0, keepdims=True)
    loss_ref[...] = turned[:, :rows]


def deal_rows(chip_grads, rows, width):
    return pl.pallas_call(
        deal_kernel,
        in_specs=[pl.BlockSpec(memory_space=pltpu.VMEM)],
        out_specs=[pl.BlockSpec(memory_space=pltpu.VMEM)] * 3,
        out_shape=[
            jax.ShapeDtypeStruct((1, rows), jnp.float32),
            jax.ShapeDtypeStruct((rows, width), jnp.float32),
            jax.ShapeDtypeStruct((rows, width), jnp.float32),
        ],
        compiler_params=pltpu.CompilerParams(vmem_limit_bytes=2 << 20),
        name="deal_rows",
    )(chip_grads)


def solution(mesh):
    fine = Mesh(mesh.devices.reshape(SIZES), AXES)
    in_specs = (P(AXES, None), P(AXES, None), P(), P())
    out_specs = (P(AXES), P(AXES, None), P(AXES, None))
    return jax.shard_map(
        on_device, mesh=fine, in_specs=in_specs, out_specs=out_specs, check_vma=False
    )
```

```python
import functools

import jax
import jax.numpy as jnp
from jax import lax
from jax.sharding import Mesh
from jax.experimental import pallas as pl
from jax.experimental.pallas import tpu as pltpu
from jax.sharding import PartitionSpec as P

epsilon = 1e-06
AXES = ("x", "yh", "z", "yl", "c")
SIZES = (4, 4, 12, 2, 2)
RUN = 3
GAIN = 16.0
LOSS_COLUMNS = 128


def places(x, y, z):
    run, step = z // RUN, z % RUN
    last, late = step // 2, run // 2
    half = (last + late) % 2
    text_place = RUN * y + step
    rank = last * (run + 2 * late) + (1 - last) * (2 * run - 2 * late + step)
    return (step, half, text_place, 6 * x + rank)


def exchange_groups():
    members = {}
    xs, yhs, zs, yls, cs = SIZES
    device = 0
    for x in range(xs):
        for yh in range(yhs):
            for z in range(zs):
                for yl in range(yls):
                    y = yh * yls + yl
                    _, half, text_place, image_place = places(x, y, z)
                    text_key = (0, x, z // RUN)
                    image_key = (1, y, half)
                    for core, key, place in ((0, text_key, text_place), (1, image_key, image_place)):
                        members.setdefault(key, []).append((place, device + core))
                    device += cs
    return [[device for _, device in sorted(members[key])] for key in sorted(members)]


def exchange(pieces):
    return lax.all_to_all(pieces, AXES, 0, 0, axis_index_groups=exchange_groups(), tiled=True)


def on_device(image_embeds, text_embeds, log_scale, bias):
    rows, width = image_embeds.shape
    batch = rows * lax.axis_size(AXES)
    chip_rows = 2 * rows
    chip_embeds = lax.all_gather(jnp.concatenate([text_embeds, image_embeds], axis=0), "c", axis=0)
    count = len(exchange_groups()[0])
    pieces, unit, inverse = unit_pieces(chip_embeds, count)
    own = exchange(pieces)
    both = lax.all_gather(own.reshape(-1, width), "c", axis=0)
    packed = pair_block(both, log_scale, bias, count).astype(jnp.float16)
    arrived = exchange(packed)
    total = jnp.sum(arrived.astype(jnp.float32), axis=0)
    chip_grads = lax.all_gather(chip_results(total, unit, inverse, batch), "c", axis=0)
    row_loss, image_grad, text_grad = deal_rows(chip_grads, rows, width)
    return (row_loss.reshape(rows), image_grad, text_grad)


def unit_kernel(chip_ref, pieces_ref, unit_ref, inverse_ref):
    count, chip_rows, _ = pieces_ref.shape
    rows = chip_rows // 2
    first, second = chip_ref[0].astype(jnp.float32), chip_ref[1].astype(jnp.float32)
    upper = lax.broadcasted_iota(jnp.int32, first.shape, 0) < rows
    text = jnp.where(upper, first, pltpu.roll(second, rows, 0))
    images = jnp.where(upper, pltpu.roll(first, rows, 0), second)
    values = jnp.where(lax.axis_index("c") == 0, text, images)
    inverse = lax.rsqrt(jnp.sum(values * values, axis=1, keepdims=True) + epsilon)
    unit = values * inverse
    low = unit.astype(jnp.bfloat16)
    for k in range(count):
        pieces_ref[k] = low
    unit_ref[...] = unit
    inverse_ref[...] = jnp.broadcast_to(inverse, unit.shape)


def unit_pieces(chip_embeds, count):
    _, chip_rows, width = chip_embeds.shape
    return pl.pallas_call(
        unit_kernel,
        in_specs=[pl.BlockSpec(memory_space=pltpu.VMEM)],
        out_specs=[pl.BlockSpec(memory_space=pltpu.VMEM)] * 3,
        out_shape=[
            jax.ShapeDtypeStruct((count, chip_rows, width), jnp.bfloat16),
            jax.ShapeDtypeStruct((chip_rows, width), jnp.float32),
            jax.ShapeDtypeStruct((chip_rows, width), jnp.float32),
        ],
        compiler_params=pltpu.CompilerParams(vmem_limit_bytes=4 << 20),
        name="unit_pieces",
    )(chip_embeds)


def results_kernel(batch, total_ref, unit_ref, inverse_ref, results_ref):
    width = unit_ref.shape[1]
    upstream = total_ref[:, :width] * (1.0 / GAIN)
    unit = unit_ref[...]
    along = jnp.sum(unit * upstream, axis=1, keepdims=True)
    results_ref[:, :width] = inverse_ref[...] * (upstream - unit * along)
    terms = total_ref[:, width:]
    both = terms + pltpu.roll(terms, LOSS_COLUMNS // 2, 1)
    results_ref[:, width:] = both * (1.0 / (GAIN * batch))


def chip_results(total, unit, inverse, batch):
    return pl.pallas_call(
        functools.partial(results_kernel, batch),
        in_specs=[pl.BlockSpec(memory_space=pltpu.VMEM)] * 3,
        out_specs=pl.BlockSpec(memory_space=pltpu.VMEM),
        out_shape=jax.ShapeDtypeStruct(total.shape, jnp.float32),
        compiler_params=pltpu.CompilerParams(vmem_limit_bytes=2 << 20),
        name="chip_results",
    )(total, unit, inverse)


def block_kernel(both_ref, log_scale_ref, bias_ref, packed_ref):
    count, chip_rows, _ = packed_ref.shape
    width = both_ref.shape[2]
    x, yh, z, yl, c = [lax.axis_index(name) for name in AXES]
    own, other = both_ref[c], both_ref[1 - c]
    step, _, text_place, image_place = places(x, yh * SIZES[3] + yl, z)
    own_place = jnp.where(c == 0, text_place, image_place)
    other_place = jnp.where(c == 0, image_place, text_place)
    pairs = (own.shape[0], other.shape[0])
    own_ids = lax.broadcasted_iota(jnp.int32, pairs, 0) - chip_rows * own_place
    other_ids = lax.broadcasted_iota(jnp.int32, pairs, 1) - chip_rows * other_place
    chips = jnp.where(step == 0, 2, 1)
    positive = (own_ids == other_ids) & (own_ids >= 0) & (own_ids < chips * chip_rows)
    counted = jnp.where(step == 1, 0.0, 1.0)
    raw_logits = lax.dot_general(
        own, other, (((1,), (1,)), ((), ())), preferred_element_type=jnp.float32
    )
    scale_value = jnp.exp(log_scale_ref[...])
    logits = scale_value * raw_logits + bias_ref[...]
    labels = jnp.where(positive, 1.0, -1.0)
    margins = -labels * logits
    softplus = jnp.maximum(margins, 0.0) + jnp.log1p(jnp.exp(-jnp.abs(margins)))
    losses = (GAIN * counted) * jnp.sum(softplus, axis=1, keepdims=True)
    coefs = ((-counted * scale_value) * labels * jax.nn.sigmoid(margins)).astype(jnp.bfloat16)
    part = jnp.dot(coefs, other, preferred_element_type=jnp.float32) * GAIN
    packed_ref[:, :, :width] = part.reshape(count, chip_rows, width)
    rounded = losses.astype(jnp.bfloat16).astype(jnp.float32)
    column = lax.broadcasted_iota(jnp.int32, (pairs[0], LOSS_COLUMNS), 1)
    columns = jnp.where(column < LOSS_COLUMNS // 2, rounded, losses - rounded)
    packed_ref[:, :, width:] = columns.reshape(count, chip_rows, LOSS_COLUMNS)


def pair_block(both, log_scale, bias, count):
    _, own_rows, width = both.shape
    return pl.pallas_call(
        block_kernel,
        in_specs=[pl.BlockSpec(memory_space=pltpu.VMEM)] * 3,
        out_specs=pl.BlockSpec(memory_space=pltpu.VMEM),
        out_shape=jax.ShapeDtypeStruct((count, own_rows // count, width + LOSS_COLUMNS), jnp.float32),
        compiler_params=pltpu.CompilerParams(vmem_limit_bytes=12 << 20),
        name="pair_block",
    )(both, log_scale.reshape(1, 1), bias.reshape(1, 1))


def deal_kernel(chip_ref, loss_ref, image_ref, text_ref):
    rows, width = image_ref.shape
    core = lax.axis_index("c")
    for kind, out_ref in ((0, text_ref), (1, image_ref)):
        out_ref[...] = jnp.where(
            core == 0, chip_ref[kind, :rows, :width], chip_ref[kind, rows:, :width]
        )
    losses = chip_ref[1, :, width:]
    row = lax.broadcasted_iota(jnp.int32, losses.shape, 0)
    column = lax.broadcasted_iota(jnp.int32, losses.shape, 1)
    turned = jnp.sum(jnp.where(row == column + rows * core, losses, 0.0), axis=0, keepdims=True)
    loss_ref[...] = turned[:, :rows]


def deal_rows(chip_grads, rows, width):
    return pl.pallas_call(
        deal_kernel,
        in_specs=[pl.BlockSpec(memory_space=pltpu.VMEM)],
        out_specs=[pl.BlockSpec(memory_space=pltpu.VMEM)] * 3,
        out_shape=[
            jax.ShapeDtypeStruct((1, rows), jnp.float32),
            jax.ShapeDtypeStruct((rows, width), jnp.float32),
            jax.ShapeDtypeStruct((rows, width), jnp.float32),
        ],
        compiler_params=pltpu.CompilerParams(vmem_limit_bytes=2 << 20),
        name="deal_rows",
    )(chip_grads)


def solution(mesh):
    fine = Mesh(mesh.devices.reshape(SIZES), AXES)
    in_specs = (P(AXES, None), P(AXES, None), P(), P())
    out_specs = (P(AXES), P(AXES, None), P(AXES, None))
    return jax.shard_map(
        on_device, mesh=fine, in_specs=in_specs, out_specs=out_specs, check_vma=False
    )
```

```python
import functools

import jax
import jax.numpy as jnp
from jax import lax
from jax.sharding import Mesh
from jax.experimental import pallas as pl
from jax.experimental.pallas import tpu as pltpu
from jax.sharding import PartitionSpec as P

epsilon = 1e-06
AXES = ("x", "yh", "z", "yl", "c")
SIZES = (4, 4, 12, 2, 2)
RUN = 3
TURN = 5
GAIN = 16.0
LOSS_COLUMNS = 128


def places(x, y, z):
    turned = (z + TURN) % SIZES[2]
    run, step = turned // RUN, turned % RUN
    last, late = step // 2, run // 2
    half = (last + late) % 2
    text_place = RUN * y + step
    rank = last * (run + 2 * late) + (1 - last) * (2 * run - 2 * late + step)
    return (run, step, half, text_place, 6 * x + rank)


def exchange_groups():
    members = {}
    xs, yhs, zs, yls, cs = SIZES
    device = 0
    for x in range(xs):
        for yh in range(yhs):
            for z in range(zs):
                for yl in range(yls):
                    y = yh * yls + yl
                    run, _, half, text_place, image_place = places(x, y, z)
                    text_key = (0, x, run)
                    image_key = (1, y, half)
                    for core, key, place in ((0, text_key, text_place), (1, image_key, image_place)):
                        members.setdefault(key, []).append((place, device + core))
                    device += cs
    return [[device for _, device in sorted(members[key])] for key in sorted(members)]


def exchange(pieces):
    return lax.all_to_all(pieces, AXES, 0, 0, axis_index_groups=exchange_groups(), tiled=True)


def on_device(image_embeds, text_embeds, log_scale, bias):
    rows, width = image_embeds.shape
    batch = rows * lax.axis_size(AXES)
    chip_rows = 2 * rows
    chip_embeds = lax.all_gather(jnp.concatenate([text_embeds, image_embeds], axis=0), "c", axis=0)
    count = len(exchange_groups()[0])
    pieces, unit, inverse = unit_pieces(chip_embeds, count)
    own = exchange(pieces)
    both = lax.all_gather(own.reshape(-1, width), "c", axis=0)
    packed = pair_block(both, log_scale, bias, count).astype(jnp.float16)
    arrived = exchange(packed)
    total = jnp.sum(arrived.astype(jnp.float32), axis=0)
    chip_grads = lax.all_gather(chip_results(total, unit, inverse, batch), "c", axis=0)
    row_loss, image_grad, text_grad = deal_rows(chip_grads, rows, width)
    return (row_loss.reshape(rows), image_grad, text_grad)


def unit_kernel(chip_ref, pieces_ref, unit_ref, inverse_ref):
    count, chip_rows, _ = pieces_ref.shape
    rows = chip_rows // 2
    first, second = chip_ref[0].astype(jnp.float32), chip_ref[1].astype(jnp.float32)
    upper = lax.broadcasted_iota(jnp.int32, first.shape, 0) < rows
    text = jnp.where(upper, first, pltpu.roll(second, rows, 0))
    images = jnp.where(upper, pltpu.roll(first, rows, 0), second)
    values = jnp.where(lax.axis_index("c") == 0, text, images)
    inverse = lax.rsqrt(jnp.sum(values * values, axis=1, keepdims=True) + epsilon)
    unit = values * inverse
    low = unit.astype(jnp.bfloat16)
    for k in range(count):
        pieces_ref[k] = low
    unit_ref[...] = unit
    inverse_ref[...] = jnp.broadcast_to(inverse, unit.shape)


def unit_pieces(chip_embeds, count):
    _, chip_rows, width = chip_embeds.shape
    return pl.pallas_call(
        unit_kernel,
        in_specs=[pl.BlockSpec(memory_space=pltpu.VMEM)],
        out_specs=[pl.BlockSpec(memory_space=pltpu.VMEM)] * 3,
        out_shape=[
            jax.ShapeDtypeStruct((count, chip_rows, width), jnp.bfloat16),
            jax.ShapeDtypeStruct((chip_rows, width), jnp.float32),
            jax.ShapeDtypeStruct((chip_rows, width), jnp.float32),
        ],
        compiler_params=pltpu.CompilerParams(vmem_limit_bytes=4 << 20),
        name="unit_pieces",
    )(chip_embeds)


def results_kernel(batch, total_ref, unit_ref, inverse_ref, results_ref):
    width = unit_ref.shape[1]
    upstream = total_ref[:, :width] * (1.0 / GAIN)
    unit = unit_ref[...]
    along = jnp.sum(unit * upstream, axis=1, keepdims=True)
    results_ref[:, :width] = inverse_ref[...] * (upstream - unit * along)
    terms = total_ref[:, width:]
    both = terms + pltpu.roll(terms, LOSS_COLUMNS // 2, 1)
    results_ref[:, width:] = both * (1.0 / (GAIN * batch))


def chip_results(total, unit, inverse, batch):
    return pl.pallas_call(
        functools.partial(results_kernel, batch),
        in_specs=[pl.BlockSpec(memory_space=pltpu.VMEM)] * 3,
        out_specs=pl.BlockSpec(memory_space=pltpu.VMEM),
        out_shape=jax.ShapeDtypeStruct(total.shape, jnp.float32),
        compiler_params=pltpu.CompilerParams(vmem_limit_bytes=2 << 20),
        name="chip_results",
    )(total, unit, inverse)


def block_kernel(both_ref, log_scale_ref, bias_ref, packed_ref):
    count, chip_rows, _ = packed_ref.shape
    width = both_ref.shape[2]
    x, yh, z, yl, c = [lax.axis_index(name) for name in AXES]
    own, other = both_ref[c], both_ref[1 - c]
    _, step, _, text_place, image_place = places(x, yh * SIZES[3] + yl, z)
    own_place = jnp.where(c == 0, text_place, image_place)
    other_place = jnp.where(c == 0, image_place, text_place)
    pairs = (own.shape[0], other.shape[0])
    own_ids = lax.broadcasted_iota(jnp.int32, pairs, 0) - chip_rows * own_place
    other_ids = lax.broadcasted_iota(jnp.int32, pairs, 1) - chip_rows * other_place
    chips = jnp.where(step == 0, 2, 1)
    positive = (own_ids == other_ids) & (own_ids >= 0) & (own_ids < chips * chip_rows)
    counted = jnp.where(step == 1, 0.0, 1.0)
    raw_logits = lax.dot_general(
        own, other, (((1,), (1,)), ((), ())), preferred_element_type=jnp.float32
    )
    scale_value = jnp.exp(log_scale_ref[...])
    logits = scale_value * raw_logits + bias_ref[...]
    labels = jnp.where(positive, 1.0, -1.0)
    margins = -labels * logits
    softplus = jnp.maximum(margins, 0.0) + jnp.log1p(jnp.exp(-jnp.abs(margins)))
    losses = (GAIN * counted) * jnp.sum(softplus, axis=1, keepdims=True)
    coefs = ((-counted * scale_value) * labels * jax.nn.sigmoid(margins)).astype(jnp.bfloat16)
    part = jnp.dot(coefs, other, preferred_element_type=jnp.float32) * GAIN
    packed_ref[:, :, :width] = part.reshape(count, chip_rows, width)
    rounded = losses.astype(jnp.bfloat16).astype(jnp.float32)
    column = lax.broadcasted_iota(jnp.int32, (pairs[0], LOSS_COLUMNS), 1)
    columns = jnp.where(column < LOSS_COLUMNS // 2, rounded, losses - rounded)
    packed_ref[:, :, width:] = columns.reshape(count, chip_rows, LOSS_COLUMNS)


def pair_block(both, log_scale, bias, count):
    _, own_rows, width = both.shape
    return pl.pallas_call(
        block_kernel,
        in_specs=[pl.BlockSpec(memory_space=pltpu.VMEM)] * 3,
        out_specs=pl.BlockSpec(memory_space=pltpu.VMEM),
        out_shape=jax.ShapeDtypeStruct((count, own_rows // count, width + LOSS_COLUMNS), jnp.float32),
        compiler_params=pltpu.CompilerParams(vmem_limit_bytes=12 << 20),
        name="pair_block",
    )(both, log_scale.reshape(1, 1), bias.reshape(1, 1))


def deal_kernel(chip_ref, loss_ref, image_ref, text_ref):
    rows, width = image_ref.shape
    core = lax.axis_index("c")
    for kind, out_ref in ((0, text_ref), (1, image_ref)):
        out_ref[...] = jnp.where(
            core == 0, chip_ref[kind, :rows, :width], chip_ref[kind, rows:, :width]
        )
    losses = chip_ref[1, :, width:]
    row = lax.broadcasted_iota(jnp.int32, losses.shape, 0)
    column = lax.broadcasted_iota(jnp.int32, losses.shape, 1)
    turned = jnp.sum(jnp.where(row == column + rows * core, losses, 0.0), axis=0, keepdims=True)
    loss_ref[...] = turned[:, :rows]


def deal_rows(chip_grads, rows, width):
    return pl.pallas_call(
        deal_kernel,
        in_specs=[pl.BlockSpec(memory_space=pltpu.VMEM)],
        out_specs=[pl.BlockSpec(memory_space=pltpu.VMEM)] * 3,
        out_shape=[
            jax.ShapeDtypeStruct((1, rows), jnp.float32),
            jax.ShapeDtypeStruct((rows, width), jnp.float32),
            jax.ShapeDtypeStruct((rows, width), jnp.float32),
        ],
        compiler_params=pltpu.CompilerParams(vmem_limit_bytes=2 << 20),
        name="deal_rows",
    )(chip_grads)


def solution(mesh):
    fine = Mesh(mesh.devices.reshape(SIZES), AXES)
    in_specs = (P(AXES, None), P(AXES, None), P(), P())
    out_specs = (P(AXES), P(AXES, None), P(AXES, None))
    return jax.shard_map(
        on_device, mesh=fine, in_specs=in_specs, out_specs=out_specs, check_vma=False
    )
```

```python
import functools

import jax
import jax.numpy as jnp
from jax import lax
from jax.sharding import Mesh
from jax.experimental import pallas as pl
from jax.experimental.pallas import tpu as pltpu
from jax.sharding import PartitionSpec as P

epsilon = 1e-06
AXES = ("x", "yh", "z", "yl", "c")
SIZES = (4, 4, 12, 2, 2)
RUN = 3
TURN = 3
GAIN = 16.0
LOSS_COLUMNS = 128


def places(x, y, z):
    turned = (z + TURN) % SIZES[2]
    run, step = turned // RUN, turned % RUN
    last, late = step // 2, run // 2
    half = (last + late) % 2
    text_place = RUN * y + step
    rank = last * (run + 2 * late) + (1 - last) * (2 * run - 2 * late + step)
    return (run, step, half, text_place, 6 * x + rank)


def exchange_groups():
    members = {}
    xs, yhs, zs, yls, cs = SIZES
    device = 0
    for x in range(xs):
        for yh in range(yhs):
            for z in range(zs):
                for yl in range(yls):
                    y = yh * yls + yl
                    run, _, half, text_place, image_place = places(x, y, z)
                    text_key = (0, x, run)
                    image_key = (1, y, half)
                    for core, key, place in ((0, text_key, text_place), (1, image_key, image_place)):
                        members.setdefault(key, []).append((place, device + core))
                    device += cs
    return [[device for _, device in sorted(members[key])] for key in sorted(members)]


def exchange(pieces):
    return lax.all_to_all(pieces, AXES, 0, 0, axis_index_groups=exchange_groups(), tiled=True)


def on_device(image_embeds, text_embeds, log_scale, bias):
    rows, width = image_embeds.shape
    batch = rows * lax.axis_size(AXES)
    chip_rows = 2 * rows
    chip_embeds = lax.all_gather(jnp.concatenate([text_embeds, image_embeds], axis=0), "c", axis=0)
    count = len(exchange_groups()[0])
    pieces, unit, inverse = unit_pieces(chip_embeds, count)
    own = exchange(pieces)
    both = lax.all_gather(own.reshape(-1, width), "c", axis=0)
    packed = pair_block(both, log_scale, bias, count).astype(jnp.float16)
    arrived = exchange(packed)
    total = jnp.sum(arrived.astype(jnp.float32), axis=0)
    chip_grads = lax.all_gather(chip_results(total, unit, inverse, batch), "c", axis=0)
    row_loss, image_grad, text_grad = deal_rows(chip_grads, rows, width)
    return (row_loss.reshape(rows), image_grad, text_grad)


def unit_kernel(chip_ref, pieces_ref, unit_ref, inverse_ref):
    count, chip_rows, _ = pieces_ref.shape
    rows = chip_rows // 2
    first, second = chip_ref[0].astype(jnp.float32), chip_ref[1].astype(jnp.float32)
    upper = lax.broadcasted_iota(jnp.int32, first.shape, 0) < rows
    text = jnp.where(upper, first, pltpu.roll(second, rows, 0))
    images = jnp.where(upper, pltpu.roll(first, rows, 0), second)
    values = jnp.where(lax.axis_index("c") == 0, text, images)
    inverse = lax.rsqrt(jnp.sum(values * values, axis=1, keepdims=True) + epsilon)
    unit = values * inverse
    low = unit.astype(jnp.bfloat16)
    for k in range(count):
        pieces_ref[k] = low
    unit_ref[...] = unit
    inverse_ref[...] = jnp.broadcast_to(inverse, unit.shape)


def unit_pieces(chip_embeds, count):
    _, chip_rows, width = chip_embeds.shape
    return pl.pallas_call(
        unit_kernel,
        in_specs=[pl.BlockSpec(memory_space=pltpu.VMEM)],
        out_specs=[pl.BlockSpec(memory_space=pltpu.VMEM)] * 3,
        out_shape=[
            jax.ShapeDtypeStruct((count, chip_rows, width), jnp.bfloat16),
            jax.ShapeDtypeStruct((chip_rows, width), jnp.float32),
            jax.ShapeDtypeStruct((chip_rows, width), jnp.float32),
        ],
        compiler_params=pltpu.CompilerParams(vmem_limit_bytes=4 << 20),
        name="unit_pieces",
    )(chip_embeds)


def results_kernel(batch, total_ref, unit_ref, inverse_ref, results_ref):
    width = unit_ref.shape[1]
    upstream = total_ref[:, :width] * (1.0 / GAIN)
    unit = unit_ref[...]
    along = jnp.sum(unit * upstream, axis=1, keepdims=True)
    results_ref[:, :width] = inverse_ref[...] * (upstream - unit * along)
    terms = total_ref[:, width:]
    both = terms + pltpu.roll(terms, LOSS_COLUMNS // 2, 1)
    results_ref[:, width:] = both * (1.0 / (GAIN * batch))


def chip_results(total, unit, inverse, batch):
    return pl.pallas_call(
        functools.partial(results_kernel, batch),
        in_specs=[pl.BlockSpec(memory_space=pltpu.VMEM)] * 3,
        out_specs=pl.BlockSpec(memory_space=pltpu.VMEM),
        out_shape=jax.ShapeDtypeStruct(total.shape, jnp.float32),
        compiler_params=pltpu.CompilerParams(vmem_limit_bytes=2 << 20),
        name="chip_results",
    )(total, unit, inverse)


def block_kernel(both_ref, log_scale_ref, bias_ref, packed_ref):
    count, chip_rows, _ = packed_ref.shape
    width = both_ref.shape[2]
    x, yh, z, yl, c = [lax.axis_index(name) for name in AXES]
    own, other = both_ref[c], both_ref[1 - c]
    _, step, _, text_place, image_place = places(x, yh * SIZES[3] + yl, z)
    own_place = jnp.where(c == 0, text_place, image_place)
    other_place = jnp.where(c == 0, image_place, text_place)
    pairs = (own.shape[0], other.shape[0])
    own_ids = lax.broadcasted_iota(jnp.int32, pairs, 0) - chip_rows * own_place
    other_ids = lax.broadcasted_iota(jnp.int32, pairs, 1) - chip_rows * other_place
    chips = jnp.where(step == 0, 2, 1)
    positive = (own_ids == other_ids) & (own_ids >= 0) & (own_ids < chips * chip_rows)
    counted = jnp.where(step == 1, 0.0, 1.0)
    raw_logits = lax.dot_general(
        own, other, (((1,), (1,)), ((), ())), preferred_element_type=jnp.float32
    )
    scale_value = jnp.exp(log_scale_ref[...])
    logits = scale_value * raw_logits + bias_ref[...]
    labels = jnp.where(positive, 1.0, -1.0)
    margins = -labels * logits
    softplus = jnp.maximum(margins, 0.0) + jnp.log1p(jnp.exp(-jnp.abs(margins)))
    losses = (GAIN * counted) * jnp.sum(softplus, axis=1, keepdims=True)
    coefs = ((-counted * scale_value) * labels * jax.nn.sigmoid(margins)).astype(jnp.bfloat16)
    part = jnp.dot(coefs, other, preferred_element_type=jnp.float32) * GAIN
    packed_ref[:, :, :width] = part.reshape(count, chip_rows, width)
    rounded = losses.astype(jnp.bfloat16).astype(jnp.float32)
    column = lax.broadcasted_iota(jnp.int32, (pairs[0], LOSS_COLUMNS), 1)
    columns = jnp.where(column < LOSS_COLUMNS // 2, rounded, losses - rounded)
    packed_ref[:, :, width:] = columns.reshape(count, chip_rows, LOSS_COLUMNS)


def pair_block(both, log_scale, bias, count):
    _, own_rows, width = both.shape
    return pl.pallas_call(
        block_kernel,
        in_specs=[pl.BlockSpec(memory_space=pltpu.VMEM)] * 3,
        out_specs=pl.BlockSpec(memory_space=pltpu.VMEM),
        out_shape=jax.ShapeDtypeStruct((count, own_rows // count, width + LOSS_COLUMNS), jnp.float32),
        compiler_params=pltpu.CompilerParams(vmem_limit_bytes=12 << 20),
        name="pair_block",
    )(both, log_scale.reshape(1, 1), bias.reshape(1, 1))


def deal_kernel(chip_ref, loss_ref, image_ref, text_ref):
    rows, width = image_ref.shape
    core = lax.axis_index("c")
    for kind, out_ref in ((0, text_ref), (1, image_ref)):
        out_ref[...] = jnp.where(
            core == 0, chip_ref[kind, :rows, :width], chip_ref[kind, rows:, :width]
        )
    losses = chip_ref[1, :, width:]
    row = lax.broadcasted_iota(jnp.int32, losses.shape, 0)
    column = lax.broadcasted_iota(jnp.int32, losses.shape, 1)
    turned = jnp.sum(jnp.where(row == column + rows * core, losses, 0.0), axis=0, keepdims=True)
    loss_ref[...] = turned[:, :rows]


def deal_rows(chip_grads, rows, width):
    return pl.pallas_call(
        deal_kernel,
        in_specs=[pl.BlockSpec(memory_space=pltpu.VMEM)],
        out_specs=[pl.BlockSpec(memory_space=pltpu.VMEM)] * 3,
        out_shape=[
            jax.ShapeDtypeStruct((1, rows), jnp.float32),
            jax.ShapeDtypeStruct((rows, width), jnp.float32),
            jax.ShapeDtypeStruct((rows, width), jnp.float32),
        ],
        compiler_params=pltpu.CompilerParams(vmem_limit_bytes=2 << 20),
        name="deal_rows",
    )(chip_grads)


def solution(mesh):
    fine = Mesh(mesh.devices.reshape(SIZES), AXES)
    in_specs = (P(AXES, None), P(AXES, None), P(), P())
    out_specs = (P(AXES), P(AXES, None), P(AXES, None))
    return jax.shard_map(
        on_device, mesh=fine, in_specs=in_specs, out_specs=out_specs, check_vma=False
    )
```

```python
import functools

import jax
import jax.numpy as jnp
from jax import lax
from jax.sharding import Mesh
from jax.experimental import pallas as pl
from jax.experimental.pallas import tpu as pltpu
from jax.sharding import PartitionSpec as P

epsilon = 1e-06
AXES = ("x", "yh", "z", "yl", "c")
SIZES = (4, 4, 12, 2, 2)
RUN = 3
TURN = 3
GAIN = 16.0
LOSS_COLUMNS = 128


def places(x, y, z):
    turned = (z + TURN) % SIZES[2]
    run, step = turned // RUN, turned % RUN
    last, late = step // 2, run // 2
    half = (last + late) % 2
    text_place = RUN * ((y + 4) % 8) + step
    rank = last * (run + 2 * late) + (1 - last) * (2 * run - 2 * late + step)
    return (run, step, half, text_place, 6 * x + rank)


def exchange_groups():
    members = {}
    xs, yhs, zs, yls, cs = SIZES
    device = 0
    for x in range(xs):
        for yh in range(yhs):
            for z in range(zs):
                for yl in range(yls):
                    y = yh * yls + yl
                    run, _, half, text_place, image_place = places(x, y, z)
                    text_key = (0, x, run)
                    image_key = (1, y, half)
                    for core, key, place in ((0, text_key, text_place), (1, image_key, image_place)):
                        members.setdefault(key, []).append((place, device + core))
                    device += cs
    return [[device for _, device in sorted(members[key])] for key in sorted(members)]


def exchange(pieces):
    return lax.all_to_all(pieces, AXES, 0, 0, axis_index_groups=exchange_groups(), tiled=True)


def on_device(image_embeds, text_embeds, log_scale, bias):
    rows, width = image_embeds.shape
    batch = rows * lax.axis_size(AXES)
    chip_rows = 2 * rows
    chip_embeds = lax.all_gather(jnp.concatenate([text_embeds, image_embeds], axis=0), "c", axis=0)
    count = len(exchange_groups()[0])
    pieces, unit, inverse = unit_pieces(chip_embeds, count)
    own = exchange(pieces)
    both = lax.all_gather(own.reshape(-1, width), "c", axis=0)
    packed = pair_block(both, log_scale, bias, count).astype(jnp.float16)
    arrived = exchange(packed)
    total = jnp.sum(arrived.astype(jnp.float32), axis=0)
    chip_grads = lax.all_gather(chip_results(total, unit, inverse, batch), "c", axis=0)
    row_loss, image_grad, text_grad = deal_rows(chip_grads, rows, width)
    return (row_loss.reshape(rows), image_grad, text_grad)


def unit_kernel(chip_ref, pieces_ref, unit_ref, inverse_ref):
    count, chip_rows, _ = pieces_ref.shape
    rows = chip_rows // 2
    first, second = chip_ref[0].astype(jnp.float32), chip_ref[1].astype(jnp.float32)
    upper = lax.broadcasted_iota(jnp.int32, first.shape, 0) < rows
    text = jnp.where(upper, first, pltpu.roll(second, rows, 0))
    images = jnp.where(upper, pltpu.roll(first, rows, 0), second)
    values = jnp.where(lax.axis_index("c") == 0, text, images)
    inverse = lax.rsqrt(jnp.sum(values * values, axis=1, keepdims=True) + epsilon)
    unit = values * inverse
    low = unit.astype(jnp.bfloat16)
    for k in range(count):
        pieces_ref[k] = low
    unit_ref[...] = unit
    inverse_ref[...] = jnp.broadcast_to(inverse, unit.shape)


def unit_pieces(chip_embeds, count):
    _, chip_rows, width = chip_embeds.shape
    return pl.pallas_call(
        unit_kernel,
        in_specs=[pl.BlockSpec(memory_space=pltpu.VMEM)],
        out_specs=[pl.BlockSpec(memory_space=pltpu.VMEM)] * 3,
        out_shape=[
            jax.ShapeDtypeStruct((count, chip_rows, width), jnp.bfloat16),
            jax.ShapeDtypeStruct((chip_rows, width), jnp.float32),
            jax.ShapeDtypeStruct((chip_rows, width), jnp.float32),
        ],
        compiler_params=pltpu.CompilerParams(vmem_limit_bytes=4 << 20),
        name="unit_pieces",
    )(chip_embeds)


def results_kernel(batch, total_ref, unit_ref, inverse_ref, results_ref):
    width = unit_ref.shape[1]
    upstream = total_ref[:, :width] * (1.0 / GAIN)
    unit = unit_ref[...]
    along = jnp.sum(unit * upstream, axis=1, keepdims=True)
    results_ref[:, :width] = inverse_ref[...] * (upstream - unit * along)
    terms = total_ref[:, width:]
    both = terms + pltpu.roll(terms, LOSS_COLUMNS // 2, 1)
    results_ref[:, width:] = both * (1.0 / (GAIN * batch))


def chip_results(total, unit, inverse, batch):
    return pl.pallas_call(
        functools.partial(results_kernel, batch),
        in_specs=[pl.BlockSpec(memory_space=pltpu.VMEM)] * 3,
        out_specs=pl.BlockSpec(memory_space=pltpu.VMEM),
        out_shape=jax.ShapeDtypeStruct(total.shape, jnp.float32),
        compiler_params=pltpu.CompilerParams(vmem_limit_bytes=2 << 20),
        name="chip_results",
    )(total, unit, inverse)


def block_kernel(both_ref, log_scale_ref, bias_ref, packed_ref):
    count, chip_rows, _ = packed_ref.shape
    width = both_ref.shape[2]
    x, yh, z, yl, c = [lax.axis_index(name) for name in AXES]
    own, other = both_ref[c], both_ref[1 - c]
    _, step, _, text_place, image_place = places(x, yh * SIZES[3] + yl, z)
    own_place = jnp.where(c == 0, text_place, image_place)
    other_place = jnp.where(c == 0, image_place, text_place)
    pairs = (own.shape[0], other.shape[0])
    own_ids = lax.broadcasted_iota(jnp.int32, pairs, 0) - chip_rows * own_place
    other_ids = lax.broadcasted_iota(jnp.int32, pairs, 1) - chip_rows * other_place
    chips = jnp.where(step == 0, 2, 1)
    positive = (own_ids == other_ids) & (own_ids >= 0) & (own_ids < chips * chip_rows)
    counted = jnp.where(step == 1, 0.0, 1.0)
    raw_logits = lax.dot_general(
        own, other, (((1,), (1,)), ((), ())), preferred_element_type=jnp.float32
    )
    scale_value = jnp.exp(log_scale_ref[...])
    logits = scale_value * raw_logits + bias_ref[...]
    labels = jnp.where(positive, 1.0, -1.0)
    margins = -labels * logits
    softplus = jnp.maximum(margins, 0.0) + jnp.log1p(jnp.exp(-jnp.abs(margins)))
    losses = (GAIN * counted) * jnp.sum(softplus, axis=1, keepdims=True)
    coefs = ((-counted * scale_value) * labels * jax.nn.sigmoid(margins)).astype(jnp.bfloat16)
    part = jnp.dot(coefs, other, preferred_element_type=jnp.float32) * GAIN
    packed_ref[:, :, :width] = part.reshape(count, chip_rows, width)
    rounded = losses.astype(jnp.bfloat16).astype(jnp.float32)
    column = lax.broadcasted_iota(jnp.int32, (pairs[0], LOSS_COLUMNS), 1)
    columns = jnp.where(column < LOSS_COLUMNS // 2, rounded, losses - rounded)
    packed_ref[:, :, width:] = columns.reshape(count, chip_rows, LOSS_COLUMNS)


def pair_block(both, log_scale, bias, count):
    _, own_rows, width = both.shape
    return pl.pallas_call(
        block_kernel,
        in_specs=[pl.BlockSpec(memory_space=pltpu.VMEM)] * 3,
        out_specs=pl.BlockSpec(memory_space=pltpu.VMEM),
        out_shape=jax.ShapeDtypeStruct((count, own_rows // count, width + LOSS_COLUMNS), jnp.float32),
        compiler_params=pltpu.CompilerParams(vmem_limit_bytes=12 << 20),
        name="pair_block",
    )(both, log_scale.reshape(1, 1), bias.reshape(1, 1))


def deal_kernel(chip_ref, loss_ref, image_ref, text_ref):
    rows, width = image_ref.shape
    core = lax.axis_index("c")
    for kind, out_ref in ((0, text_ref), (1, image_ref)):
        out_ref[...] = jnp.where(
            core == 0, chip_ref[kind, :rows, :width], chip_ref[kind, rows:, :width]
        )
    losses = chip_ref[1, :, width:]
    row = lax.broadcasted_iota(jnp.int32, losses.shape, 0)
    column = lax.broadcasted_iota(jnp.int32, losses.shape, 1)
    turned = jnp.sum(jnp.where(row == column + rows * core, losses, 0.0), axis=0, keepdims=True)
    loss_ref[...] = turned[:, :rows]


def deal_rows(chip_grads, rows, width):
    return pl.pallas_call(
        deal_kernel,
        in_specs=[pl.BlockSpec(memory_space=pltpu.VMEM)],
        out_specs=[pl.BlockSpec(memory_space=pltpu.VMEM)] * 3,
        out_shape=[
            jax.ShapeDtypeStruct((1, rows), jnp.float32),
            jax.ShapeDtypeStruct((rows, width), jnp.float32),
            jax.ShapeDtypeStruct((rows, width), jnp.float32),
        ],
        compiler_params=pltpu.CompilerParams(vmem_limit_bytes=2 << 20),
        name="deal_rows",
    )(chip_grads)


def solution(mesh):
    fine = Mesh(mesh.devices.reshape(SIZES), AXES)
    in_specs = (P(AXES, None), P(AXES, None), P(), P())
    out_specs = (P(AXES), P(AXES, None), P(AXES, None))
    return jax.shard_map(
        on_device, mesh=fine, in_specs=in_specs, out_specs=out_specs, check_vma=False
    )
```
